32 devices in a mesh: parts: 2 (over y), tensor: 4 (over z), dp: 4 (over x, core).
Axes of the slice: x: 2, y: 2, z: 4, core: 2. Of those that a mesh axis runs over, the one named last changes fastest.
Arguments:
- x_up: bfloat16 [16384, 4096], P(('parts', 'dp'), 'tensor'), parts along dimension 0, may hold values from -6 to 6
- g_up: bfloat16 [16384, 14336], P(('parts', 'dp'), 'tensor'), parts along dimension 0, may hold values from -6 to 6
- h_down: bfloat16 [16384, 14336], P(('parts', 'dp'), 'tensor'), parts along dimension 0, may hold values from -6 to 6
- g_down: bfloat16 [16384, 4096], P(('parts', 'dp'), 'tensor'), parts along dimension 0, may hold values from -6 to 6
- proj_model: bfloat16 [4096, 128], P('tensor'), may hold values from -0.09375 to 0.09375
- proj_hidden: bfloat16 [14336, 128], P('tensor'), may hold values from -0.046875 to 0.046875
- lengths: int32 [16], P(('parts', 'dp')), parts along dimension 0, may hold values from 256 to 1024, as said below
- bank: bfloat16 [1024, 8192], P(None, 'tensor'), may hold values from -2.390625 to 2.390625
Outputs:
- scores: float32 [16, 1024], P(('parts', 'dp'), 'tensor'), parts along dimension 0
The draws below stay inside these ranges and needn't reach their ends.
There are 2 independent parts, one for each index of `parts`. The reference program is written for one: setup_inputs(seed, part) draws one part's arguments, and reference() takes and returns one part's arrays. A program takes and returns all parts, laid end to end along the dimension named above; an argument that names none is the same for every part. Nothing has to cross between parts.
Inputs may be any that keep to these rules, and one draw needn't show every extreme that they name: `lengths`: at least 256 live tokens in every sequence, and in every draw some sequence is entirely live.
All inputs are finite; a program needn't handle non-finite values.
Results may differ from the reference program's by a relative error of at most 0.0029.
Values sent between devices are 32-bit elements; how exact they have to be, the bound alone decides.
A program may use at most 128 MiB of HBM per device.

```python
import jax
import jax.numpy as jnp
from jax import lax

D = 4096
FF = 14336
PROJ = 64
NQ = 1024
SEQ_LEN = 1024
SEQS = 8
TOKENS = 8192
FEAT = 8192


def draw_lengths(key, part):
    key = jax.random.fold_in(key, 7)
    first_key, second_key = jax.random.split(key)
    drawn_lengths = jax.random.randint(first_key, (SEQS,), SEQ_LEN // 4, SEQ_LEN + 1, dtype=jnp.int32)
    chosen = jax.random.randint(second_key, (), 0, SEQS, dtype=jnp.int32)
    return jnp.where(jnp.arange(SEQS, dtype=jnp.int32) == chosen, SEQ_LEN, drawn_lengths).astype(jnp.int32)


def with_spikes(entries, own_key, source, target, parts, factor):
    owner, partner = [(jnp.arange(entries.shape[dim]) // (entries.shape[dim] // parts)).reshape([-1 if axis == dim else 1 for axis in range(entries.ndim)]) for dim in (source, target)]
    chosen = jax.random.permutation(own_key, parts)[partner]
    strong = (owner == chosen) | (owner == (partner + parts // 2) % parts)
    return jnp.where(strong, factor * entries, entries)


def steps_of(key, shape, pieces, least, top_value):
    def one(dim, parts):
        draws = jax.random.uniform(jax.random.fold_in(jax.random.fold_in(key, 6), dim), (parts,), jnp.float32, least / len(pieces), top_value / len(pieces))
        return jnp.repeat(jnp.exp(draws), shape[dim] // parts).reshape((-1,) + (1,) * (len(shape) - dim - 1))

    loudness = one(*pieces[0])
    for cut in pieces[1:]:
        loudness = loudness * one(*cut)
    return loudness


def noise(stream_key, dims, spread, reach, pieces=(), kind=jnp.bfloat16):
    drawn = spread * jax.random.normal(stream_key, dims, jnp.float32)
    if pieces:
        drawn = drawn * steps_of(stream_key, dims, pieces, -0.22, 0.18)
    return jnp.clip(drawn, -reach, reach).astype(kind)


def noise_with(key, dims, deviation, bound, shards, heavy, kind=jnp.bfloat16):
    drawn = deviation * jax.random.normal(key, dims, jnp.float32)
    if shards:
        drawn = drawn * steps_of(key, dims, shards, -0.22, 0.18)
    return jnp.clip(with_spikes(drawn, jax.random.fold_in(key, 3), *heavy), -bound, bound).astype(kind)


def setup_inputs(seed: int = 0, part: int = 0) -> dict:
    arg_keys = jax.random.split(jax.random.key(seed), 9)
    part_splits = jax.random.split(jax.random.fold_in(arg_keys[8], part), 9)
    x_up = noise(part_splits[0], (TOKENS, D), 1.0, 6.0, ((0, 4), (1, 4)))
    g_up = noise(part_splits[1], (TOKENS, FF), 1.0, 6.0, ((0, 4), (1, 4)))
    h_down = noise(part_splits[2], (TOKENS, FF), 1.0, 6.0, ((0, 4), (1, 4)))
    g_down = noise(part_splits[3], (TOKENS, D), 1.0, 6.0, ((0, 4), (1, 4)))
    proj_model = noise(arg_keys[4], (D, 2 * PROJ), D ** -0.5, 0.09375, ((0, 4),))
    proj_hidden = noise(arg_keys[5], (FF, 2 * PROJ), FF ** -0.5, 0.046875, ((0, 4),))
    lengths = draw_lengths(jax.random.fold_in(jax.random.fold_in(arg_keys[8], part), 71), part)
    bank = noise_with(arg_keys[7], (NQ, FEAT), 0.3, 2.390625, ((1, 4),), (1, 0, 4, 2.0))
    return {"x_up": x_up, "g_up": g_up, "h_down": h_down, "g_down": g_down, "proj_model": proj_model, "proj_hidden": proj_hidden, "lengths": lengths, "bank": bank}


def projected(activations, projection):
    return jnp.dot(activations, projection, preferred_element_type=jnp.float32)


def reference(x_up, g_up, h_down, g_down, proj_model, proj_hidden, lengths, bank):
    up_input = projected(x_up, proj_model[:, :PROJ])
    up_output = projected(g_up, proj_hidden[:, :PROJ])
    down_input = projected(h_down, proj_hidden[:, PROJ:])
    down_output = projected(g_down, proj_model[:, PROJ:])
    position = jnp.arange(SEQ_LEN, dtype=jnp.int32)
    live_mask = (position[None, :] < lengths[:, None]).astype(jnp.float32).reshape(TOKENS, 1)
    counts = lengths.astype(jnp.float32)
    blocks = []
    for inputs, outputs in ((up_input, up_output), (down_input, down_output)):
        masked = outputs * live_mask
        outer_sum = jnp.einsum("spi,spj->sij", inputs.reshape(SEQS, SEQ_LEN, PROJ), masked.reshape(SEQS, SEQ_LEN, PROJ), precision=lax.Precision.HIGHEST, preferred_element_type=jnp.float32)
        blocks.append((outer_sum / counts[:, None, None]).reshape(SEQS, PROJ * PROJ))
    features = jnp.concatenate(blocks, axis=1).astype(jnp.bfloat16)
    return jnp.dot(features, bank.T, preferred_element_type=jnp.float32)
```

```python
import functools

import jax
import jax.numpy as jnp
from jax import lax
from jax.experimental import pallas as pl
from jax.experimental.pallas import tpu as pltpu
from jax.sharding import PartitionSpec as P

PROJ = 64
CHUNK = 64
LAG = 2
AHEAD = 3
MESH = pl.DeviceIdType.MESH


def kernel(
    n,
    x_hbm, g_hbm, h_hbm, d_hbm, pm_hbm, ph_hbm, len_ref, bank_hbm,
    out_ref,
    xb, gb, hb, db, pm, ph, bank,
    own, got, acc, feat_out, feat_in, flat, part, part_in,
    row_sem, map_sem, send_sem, recv_sem, feat_send, feat_recv, part_send, part_recv,
):
    me = lax.axis_index("tensor")
    left, right = lax.rem(me + n - 1, n), lax.rem(me + 1, n)
    half = x_hbm.shape[0] // 2
    chunks = half // CHUNK
    queries = bank_hbm.shape[0] // n

    barrier = pltpu.get_barrier_semaphore()
    for j in range(1, n):
        pl.semaphore_signal(
            barrier, inc=1, device_id={"tensor": lax.rem(me + j, n)}, device_id_type=MESH
        )

    pairs = ((x_hbm, xb), (g_hbm, gb), (h_hbm, hb), (d_hbm, db))

    def row_copy(a, side, s):
        src, dst = pairs[a]
        return pltpu.make_async_copy(
            src.at[pl.ds(side * half + s * CHUNK, CHUNK)],
            dst.at[s, pl.ds(side * CHUNK, CHUNK)],
            row_sem.at[2 * a + side, s],
        )

    def fetch(s):
        for a in range(4):
            for side in range(2):
                row_copy(a, side, s).start()

    pm_copy = pltpu.make_async_copy(pm_hbm, pm, map_sem.at[0])
    ph_copy = pltpu.make_async_copy(ph_hbm, ph, map_sem.at[1])
    bank_copy = pltpu.make_async_copy(bank_hbm, bank, map_sem.at[2])
    pm_copy.start()
    ph_copy.start()
    for s in range(AHEAD):
        fetch(s)
    acc[...] = jnp.zeros_like(acc)
    flat[...] = jnp.zeros_like(flat)
    pl.semaphore_wait(barrier, n - 1)
    pm_copy.wait()
    ph_copy.wait()

    def chain_copy(side, k):
        return pltpu.make_async_remote_copy(
            src_ref=own.at[side, k],
            dst_ref=got.at[side, k],
            send_sem=send_sem.at[side, k],
            recv_sem=recv_sem.at[side, k],
            device_id={"tensor": left if side == 0 else right},
            device_id_type=MESH,
        )

    first = (n - 1, 0)
    last = (0, n - 1)
    lags = ((n - 1 - me) * LAG, me * LAG)

    def outer(side, k):
        both = own[side, k]
        position = k * CHUNK + lax.broadcasted_iota(jnp.int32, (CHUNK, 128), 0)
        outputs = jnp.where(position < len_ref[side], both[:, 128:], 0.0)
        acc[...] += lax.dot_general(
            both[:, :128], outputs, (((0,), (0,)), ((), ())),
            precision=lax.Precision.HIGHEST, preferred_element_type=jnp.float32,
        )

    def step(s, carry):
        @pl.when(s + AHEAD < chunks)
        def _():
            fetch(s + AHEAD)

        @pl.when(s == chunks - AHEAD)
        def _():
            bank_copy.start()

        @pl.when(s < chunks)
        def _():
            for a in range(4):
                for side in range(2):
                    row_copy(a, side, s).wait()
            low = lax.broadcasted_iota(jnp.int32, (2 * CHUNK, 128), 1) < PROJ
            dot = functools.partial(jnp.dot, preferred_element_type=jnp.float32)
            inputs = jnp.where(low, dot(xb[s], pm[...]), dot(hb[s], ph[...]))
            outputs = jnp.where(low, dot(gb[s], ph[...]), dot(db[s], pm[...]))
            for side in range(2):
                rows = slice(side * CHUNK, (side + 1) * CHUNK)
                own[side, s, :, :128] = inputs[rows]
                own[side, s, :, 128:] = outputs[rows]

                @pl.when(me == first[side])
                def _():
                    chain_copy(side, s).start()

        for side in range(2):
            k = s - lags[side]

            @pl.when((k >= 0) & (k < chunks) & (me != first[side]))
            def _():
                chain_copy(side, k).wait_recv()
                own[side, k] = own[side, k] + got[side, k]

                @pl.when(me != last[side])
                def _():
                    chain_copy(side, k).start()

                @pl.when(me == last[side])
                def _():
                    outer(side, k)

        return carry

    lax.fori_loop(0, chunks + (n - 1) * LAG, step, 0)

    def feat_copy(side, t):
        return pltpu.make_async_remote_copy(
            src_ref=feat_out.at[t],
            dst_ref=feat_in.at[side],
            send_sem=feat_send.at[t],
            recv_sem=feat_recv.at[side],
            device_id={"tensor": t},
            device_id_type=MESH,
        )

    rows = feat_out.shape[1]
    for side in range(2):
        @pl.when(me == last[side])
        def _():
            count = len_ref[side].astype(jnp.float32)
            even = acc[pl.ds(0, PROJ, stride=2), :]
            odd = acc[pl.ds(1, PROJ, stride=2), :]
            low = lax.broadcasted_iota(jnp.int32, (PROJ // 2, 128), 1) < PROJ
            up = jnp.where(low, even[: PROJ // 2], pltpu.roll(odd, PROJ, 1)[: PROJ // 2])
            down = jnp.where(low, pltpu.roll(even, PROJ, 1)[PROJ // 2 :], odd[PROJ // 2 :])
            features = jnp.concatenate([up, down], axis=0) / count
            for t in range(n):
                feat_out[t] = features[t * rows : (t + 1) * rows]
            for t in range(n):
                if t != last[side]:
                    feat_copy(side, t).start()
            feat_in[side] = feat_out[last[side]]

        @pl.when(me != last[side])
        def _():
            feat_copy(side, me).wait_recv()

    for side in range(2):
        for r in range(rows):
            flat[side : side + 1, r * 128 : (r + 1) * 128] = feat_in[side, r : r + 1, :]
    features = flat[...].astype(jnp.bfloat16)
    bank_copy.wait()

    def part_copy(j):
        t = lax.rem(me + j, n)
        return pltpu.make_async_remote_copy(
            src_ref=part.at[t],
            dst_ref=part_in.at[me],
            send_sem=part_send.at[j],
            recv_sem=part_recv.at[me],
            device_id={"tensor": t},
            device_id_type=MESH,
        )

    for j in [*range(1, n), 0]:
        t = lax.rem(me + j, n)
        scores = lax.dot_general(
            bank[pl.ds(pl.multiple_of(t * queries, queries), queries), :], features,
            (((1,), (1,)), ((), ())), preferred_element_type=jnp.float32,
        )
        part[t] = scores.T
        if j:
            part_copy(j).start()
    total = part[me]
    for j in range(1, n):
        source = lax.rem(me + j, n)
        pltpu.make_async_remote_copy(
            src_ref=part.at[source],
            dst_ref=part_in.at[source],
            send_sem=part_send.at[j],
            recv_sem=part_recv.at[source],
            device_id={"tensor": source},
            device_id_type=MESH,
        ).wait_recv()
        total = total + part_in[source]
    out_ref[...] = total[: out_ref.shape[0]]

    for side in range(2):
        @pl.when(me != last[side])
        def _():
            def sent(k, carry):
                chain_copy(side, k).wait_send()
                return carry

            lax.fori_loop(0, chunks, sent, 0)

        @pl.when(me == last[side])
        def _():
            for t in range(n):
                if t != last[side]:
                    feat_copy(side, t).wait_send()
    for j in range(1, n):
        part_copy(j).wait_send()


def per_device(n, x_up, g_up, h_down, g_down, proj_model, proj_hidden, lengths, bank):
    chunks = x_up.shape[0] // (2 * CHUNK)
    nq, feat_dev = bank.shape
    bf16, f32 = jnp.bfloat16, jnp.float32
    dma = pltpu.SemaphoreType.DMA
    hbm = pl.BlockSpec(memory_space=pl.ANY)
    tall = 2 * CHUNK
    return pl.pallas_call(
        functools.partial(kernel, n),
        out_shape=jax.ShapeDtypeStruct((lengths.shape[0], nq // n), f32),
        in_specs=[hbm] * 6 + [pl.BlockSpec(memory_space=pltpu.SMEM), hbm],
        out_specs=pl.BlockSpec(memory_space=pltpu.VMEM),
        scratch_shapes=[
            pltpu.VMEM((chunks, tall, x_up.shape[1]), bf16),
            pltpu.VMEM((chunks, tall, g_up.shape[1]), bf16),
            pltpu.VMEM((chunks, tall, h_down.shape[1]), bf16),
            pltpu.VMEM((chunks, tall, g_down.shape[1]), bf16),
            pltpu.VMEM(proj_model.shape, bf16),
            pltpu.VMEM(proj_hidden.shape, bf16),
            pltpu.VMEM(bank.shape, bf16),
            pltpu.VMEM((2, chunks, CHUNK, 256), f32),
            pltpu.VMEM((2, chunks, CHUNK, 256), f32),
            pltpu.VMEM((128, 128), f32),
            pltpu.VMEM((n, feat_dev // 128, 128), f32),
            pltpu.VMEM((2, feat_dev // 128, 128), f32),
            pltpu.VMEM((8, feat_dev), f32),
            pltpu.VMEM((n, 8, nq // n), f32),
            pltpu.VMEM((n, 8, nq // n), f32),
            dma((8, chunks)),
            dma((3,)),
            dma((2, chunks)),
            dma((2, chunks)),
            dma((n,)),
            dma((2,)),
            dma((n,)),
            dma((n,)),
        ],
        compiler_params=pltpu.CompilerParams(
            collective_id=0, has_side_effects=True, vmem_limit_bytes=58 * 1024 * 1024
        ),
        name="grad_scores",
    )(x_up, g_up, h_down, g_down, proj_model, proj_hidden, lengths, bank)


def solution(mesh):
    in_specs = (
        P(("parts", "dp"), "tensor"),
        P(("parts", "dp"), "tensor"),
        P(("parts", "dp"), "tensor"),
        P(("parts", "dp"), "tensor"),
        P("tensor", None),
        P("tensor", None),
        P(("parts", "dp")),
        P(None, "tensor"),
    )
    return jax.shard_map(
        functools.partial(per_device, mesh.shape["tensor"]),
        mesh=mesh,
        in_specs=in_specs,
        out_specs=P(("parts", "dp"), "tensor"),
        check_vma=False,
    )
```

```python
import functools

import jax
import jax.numpy as jnp
from jax import lax
from jax.experimental import pallas as pl
from jax.experimental.pallas import tpu as pltpu
from jax.sharding import PartitionSpec as P

PROJ = 64
CHUNK = 64
LAG = 3
AHEAD = 3
MESH = pl.DeviceIdType.MESH


def kernel(
    n,
    x_hbm, g_hbm, h_hbm, d_hbm, pm_hbm, ph_hbm, len_ref, bank_hbm,
    out_ref,
    xb, gb, hb, db, pm, ph, bank,
    own, got, acc, feat_out, feat_in, flat, part, part_in,
    row_sem, map_sem, send_sem, recv_sem, feat_send, feat_recv, part_send, part_recv,
):
    me = lax.axis_index("tensor")
    left, right = lax.rem(me + n - 1, n), lax.rem(me + 1, n)
    half = x_hbm.shape[0] // 2
    chunks = half // CHUNK
    queries = bank_hbm.shape[0] // n

    barrier = pltpu.get_barrier_semaphore()
    for j in range(1, n):
        pl.semaphore_signal(
            barrier, inc=1, device_id={"tensor": lax.rem(me + j, n)}, device_id_type=MESH
        )

    pairs = ((x_hbm, xb), (g_hbm, gb), (h_hbm, hb), (d_hbm, db))

    def row_copy(a, side, s):
        src, dst = pairs[a]
        return pltpu.make_async_copy(
            src.at[pl.ds(side * half + s * CHUNK, CHUNK)],
            dst.at[s, pl.ds(side * CHUNK, CHUNK)],
            row_sem.at[2 * a + side, s],
        )

    def fetch(s):
        for a in range(4):
            for side in range(2):
                row_copy(a, side, s).start()

    pm_copy = pltpu.make_async_copy(pm_hbm, pm, map_sem.at[0])
    ph_copy = pltpu.make_async_copy(ph_hbm, ph, map_sem.at[1])
    bank_copy = pltpu.make_async_copy(bank_hbm, bank, map_sem.at[2])
    pm_copy.start()
    ph_copy.start()
    for s in range(AHEAD):
        fetch(s)
    acc[...] = jnp.zeros_like(acc)
    flat[...] = jnp.zeros_like(flat)
    pl.semaphore_wait(barrier, n - 1)
    pm_copy.wait()
    ph_copy.wait()

    def chain_copy(side, k):
        return pltpu.make_async_remote_copy(
            src_ref=own.at[side, k],
            dst_ref=got.at[side, k],
            send_sem=send_sem.at[side, k],
            recv_sem=recv_sem.at[side, k],
            device_id={"tensor": left if side == 0 else right},
            device_id_type=MESH,
        )

    first = (n - 1, 0)
    last = (0, n - 1)
    lags = ((n - 1 - me) * LAG, me * LAG)

    def outer(side, k):
        both = own[side, k]
        position = k * CHUNK + lax.broadcasted_iota(jnp.int32, (CHUNK, 128), 0)
        outputs = jnp.where(position < len_ref[side], both[:, 128:], 0.0)
        acc[...] += lax.dot_general(
            both[:, :128], outputs, (((0,), (0,)), ((), ())),
            precision=lax.Precision.HIGHEST, preferred_element_type=jnp.float32,
        )

    def step(s, carry):
        @pl.when(s + AHEAD < chunks)
        def _():
            fetch(s + AHEAD)

        @pl.when(s == chunks - AHEAD)
        def _():
            bank_copy.start()

        @pl.when(s < chunks)
        def _():
            for a in range(4):
                for side in range(2):
                    row_copy(a, side, s).wait()
            low = lax.broadcasted_iota(jnp.int32, (2 * CHUNK, 128), 1) < PROJ
            dot = functools.partial(jnp.dot, preferred_element_type=jnp.float32)
            inputs = jnp.where(low, dot(xb[s], pm[...]), dot(hb[s], ph[...]))
            outputs = jnp.where(low, dot(gb[s], ph[...]), dot(db[s], pm[...]))
            for side in range(2):
                rows = slice(side * CHUNK, (side + 1) * CHUNK)
                own[side, s, :, :128] = inputs[rows]
                own[side, s, :, 128:] = outputs[rows]

                @pl.when(me == first[side])
                def _():
                    chain_copy(side, s).start()

        for side in range(2):
            k = s - lags[side]

            @pl.when((k >= 0) & (k < chunks) & (me != first[side]))
            def _():
                chain_copy(side, k).wait_recv()
                own[side, k] = own[side, k] + got[side, k]

                @pl.when(me != last[side])
                def _():
                    chain_copy(side, k).start()

                @pl.when(me == last[side])
                def _():
                    outer(side, k)

        return carry

    lax.fori_loop(0, chunks + (n - 1) * LAG, step, 0)

    def feat_copy(side, t):
        return pltpu.make_async_remote_copy(
            src_ref=feat_out.at[t],
            dst_ref=feat_in.at[side],
            send_sem=feat_send.at[t],
            recv_sem=feat_recv.at[side],
            device_id={"tensor": t},
            device_id_type=MESH,
        )

    rows = feat_out.shape[1]
    for side in range(2):
        @pl.when(me == last[side])
        def _():
            count = len_ref[side].astype(jnp.float32)
            even = acc[pl.ds(0, PROJ, stride=2), :]
            odd = acc[pl.ds(1, PROJ, stride=2), :]
            low = lax.broadcasted_iota(jnp.int32, (PROJ // 2, 128), 1) < PROJ
            up = jnp.where(low, even[: PROJ // 2], pltpu.roll(odd, PROJ, 1)[: PROJ // 2])
            down = jnp.where(low, pltpu.roll(even, PROJ, 1)[PROJ // 2 :], odd[PROJ // 2 :])
            features = jnp.concatenate([up, down], axis=0) / count
            for t in range(n):
                feat_out[t] = features[t * rows : (t + 1) * rows]
            for t in range(n):
                if t != last[side]:
                    feat_copy(side, t).start()
            feat_in[side] = feat_out[last[side]]

        @pl.when(me != last[side])
        def _():
            feat_copy(side, me).wait_recv()

    for side in range(2):
        for r in range(rows):
            flat[side : side + 1, r * 128 : (r + 1) * 128] = feat_in[side, r : r + 1, :]
    features = flat[...].astype(jnp.bfloat16)
    bank_copy.wait()

    def part_copy(j):
        t = lax.rem(me + j, n)
        return pltpu.make_async_remote_copy(
            src_ref=part.at[t],
            dst_ref=part_in.at[me],
            send_sem=part_send.at[j],
            recv_sem=part_recv.at[me],
            device_id={"tensor": t},
            device_id_type=MESH,
        )

    for j in [*range(1, n), 0]:
        t = lax.rem(me + j, n)
        scores = lax.dot_general(
            bank[pl.ds(pl.multiple_of(t * queries, queries), queries), :], features,
            (((1,), (1,)), ((), ())), preferred_element_type=jnp.float32,
        )
        part[t] = scores.T
        if j:
            part_copy(j).start()
    total = part[me]
    for j in range(1, n):
        source = lax.rem(me + j, n)
        pltpu.make_async_remote_copy(
            src_ref=part.at[source],
            dst_ref=part_in.at[source],
            send_sem=part_send.at[j],
            recv_sem=part_recv.at[source],
            device_id={"tensor": source},
            device_id_type=MESH,
        ).wait_recv()
        total = total + part_in[source]
    out_ref[...] = total[: out_ref.shape[0]]

    for side in range(2):
        @pl.when(me != last[side])
        def _():
            def sent(k, carry):
                chain_copy(side, k).wait_send()
                return carry

            lax.fori_loop(0, chunks, sent, 0)

        @pl.when(me == last[side])
        def _():
            for t in range(n):
                if t != last[side]:
                    feat_copy(side, t).wait_send()
    for j in range(1, n):
        part_copy(j).wait_send()


def per_device(n, x_up, g_up, h_down, g_down, proj_model, proj_hidden, lengths, bank):
    chunks = x_up.shape[0] // (2 * CHUNK)
    nq, feat_dev = bank.shape
    bf16, f32 = jnp.bfloat16, jnp.float32
    dma = pltpu.SemaphoreType.DMA
    hbm = pl.BlockSpec(memory_space=pl.ANY)
    tall = 2 * CHUNK
    return pl.pallas_call(
        functools.partial(kernel, n),
        out_shape=jax.ShapeDtypeStruct((lengths.shape[0], nq // n), f32),
        in_specs=[hbm] * 6 + [pl.BlockSpec(memory_space=pltpu.SMEM), hbm],
        out_specs=pl.BlockSpec(memory_space=pltpu.VMEM),
        scratch_shapes=[
            pltpu.VMEM((chunks, tall, x_up.shape[1]), bf16),
            pltpu.VMEM((chunks, tall, g_up.shape[1]), bf16),
            pltpu.VMEM((chunks, tall, h_down.shape[1]), bf16),
            pltpu.VMEM((chunks, tall, g_down.shape[1]), bf16),
            pltpu.VMEM(proj_model.shape, bf16),
            pltpu.VMEM(proj_hidden.shape, bf16),
            pltpu.VMEM(bank.shape, bf16),
            pltpu.VMEM((2, chunks, CHUNK, 256), f32),
            pltpu.VMEM((2, chunks, CHUNK, 256), f32),
            pltpu.VMEM((128, 128), f32),
            pltpu.VMEM((n, feat_dev // 128, 128), f32),
            pltpu.VMEM((2, feat_dev // 128, 128), f32),
            pltpu.VMEM((8, feat_dev), f32),
            pltpu.VMEM((n, 8, nq // n), f32),
            pltpu.VMEM((n, 8, nq // n), f32),
            dma((8, chunks)),
            dma((3,)),
            dma((2, chunks)),
            dma((2, chunks)),
            dma((n,)),
            dma((2,)),
            dma((n,)),
            dma((n,)),
        ],
        compiler_params=pltpu.CompilerParams(
            collective_id=0, has_side_effects=True, vmem_limit_bytes=58 * 1024 * 1024
        ),
        name="grad_scores",
    )(x_up, g_up, h_down, g_down, proj_model, proj_hidden, lengths, bank)


def solution(mesh):
    in_specs = (
        P(("parts", "dp"), "tensor"),
        P(("parts", "dp"), "tensor"),
        P(("parts", "dp"), "tensor"),
        P(("parts", "dp"), "tensor"),
        P("tensor", None),
        P("tensor", None),
        P(("parts", "dp")),
        P(None, "tensor"),
    )
    return jax.shard_map(
        functools.partial(per_device, mesh.shape["tensor"]),
        mesh=mesh,
        in_specs=in_specs,
        out_specs=P(("parts", "dp"), "tensor"),
        check_vma=False,
    )
```

```python
import functools

import jax
import jax.numpy as jnp
from jax import lax
from jax.experimental import pallas as pl
from jax.experimental.pallas import tpu as pltpu
from jax.sharding import PartitionSpec as P

PROJ = 64
CHUNK = 64
LAG = 3
AHEAD = 2
MESH = pl.DeviceIdType.MESH


def kernel(
    n,
    x_hbm, g_hbm, h_hbm, d_hbm, pm_hbm, ph_hbm, len_ref, bank_hbm,
    out_ref,
    xb, gb, hb, db, pm, ph, bank,
    own, got, acc, feat_out, feat_in, flat, part, part_in,
    row_sem, map_sem, send_sem, recv_sem, feat_send, feat_recv, part_send, part_recv,
):
    me = lax.axis_index("tensor")
    left, right = lax.rem(me + n - 1, n), lax.rem(me + 1, n)
    half = x_hbm.shape[0] // 2
    chunks = half // CHUNK
    queries = bank_hbm.shape[0] // n

    barrier = pltpu.get_barrier_semaphore()
    for j in range(1, n):
        pl.semaphore_signal(
            barrier, inc=1, device_id={"tensor": lax.rem(me + j, n)}, device_id_type=MESH
        )

    pairs = ((x_hbm, xb), (g_hbm, gb), (h_hbm, hb), (d_hbm, db))

    def row_copy(a, side, s):
        src, dst = pairs[a]
        return pltpu.make_async_copy(
            src.at[pl.ds(side * half + s * CHUNK, CHUNK)],
            dst.at[s, pl.ds(side * CHUNK, CHUNK)],
            row_sem.at[2 * a + side, s],
        )

    def fetch(s):
        for a in range(4):
            for side in range(2):
                row_copy(a, side, s).start()

    pm_copy = pltpu.make_async_copy(pm_hbm, pm, map_sem.at[0])
    ph_copy = pltpu.make_async_copy(ph_hbm, ph, map_sem.at[1])
    bank_copy = pltpu.make_async_copy(bank_hbm, bank, map_sem.at[2])
    pm_copy.start()
    ph_copy.start()
    for s in range(AHEAD):
        fetch(s)
    acc[...] = jnp.zeros_like(acc)
    flat[...] = jnp.zeros_like(flat)
    pl.semaphore_wait(barrier, n - 1)
    pm_copy.wait()
    ph_copy.wait()

    def chain_copy(side, k):
        return pltpu.make_async_remote_copy(
            src_ref=own.at[side, k],
            dst_ref=got.at[side, k],
            send_sem=send_sem.at[side, k],
            recv_sem=recv_sem.at[side, k],
            device_id={"tensor": left if side == 0 else right},
            device_id_type=MESH,
        )

    first = (n - 1, 0)
    last = (0, n - 1)
    lags = ((n - 1 - me) * LAG, me * LAG)

    def outer(side, k):
        both = own[side, k]
        position = k * CHUNK + lax.broadcasted_iota(jnp.int32, (CHUNK, 128), 0)
        outputs = jnp.where(position < len_ref[side], both[:, 128:], 0.0)
        acc[...] += lax.dot_general(
            both[:, :128], outputs, (((0,), (0,)), ((), ())),
            precision=lax.Precision.HIGHEST, preferred_element_type=jnp.float32,
        )

    def step(s, carry):
        @pl.when(s + AHEAD < chunks)
        def _():
            fetch(s + AHEAD)

        @pl.when(s == chunks - AHEAD)
        def _():
            bank_copy.start()

        @pl.when(s < chunks)
        def _():
            for a in range(4):
                for side in range(2):
                    row_copy(a, side, s).wait()
            low = lax.broadcasted_iota(jnp.int32, (2 * CHUNK, 128), 1) < PROJ
            dot = functools.partial(jnp.dot, preferred_element_type=jnp.float32)
            inputs = jnp.where(low, dot(xb[s], pm[...]), dot(hb[s], ph[...]))
            outputs = jnp.where(low, dot(gb[s], ph[...]), dot(db[s], pm[...]))
            for side in range(2):
                rows = slice(side * CHUNK, (side + 1) * CHUNK)
                own[side, s, :, :128] = inputs[rows]
                own[side, s, :, 128:] = outputs[rows]

                @pl.when(me == first[side])
                def _():
                    chain_copy(side, s).start()

        for side in range(2):
            k = s - lags[side]

            @pl.when((k >= 0) & (k < chunks) & (me != first[side]))
            def _():
                chain_copy(side, k).wait_recv()
                own[side, k] = own[side, k] + got[side, k]

                @pl.when(me != last[side])
                def _():
                    chain_copy(side, k).start()

                @pl.when(me == last[side])
                def _():
                    outer(side, k)

        return carry

    lax.fori_loop(0, chunks + (n - 1) * LAG, step, 0)

    def feat_copy(side, t):
        return pltpu.make_async_remote_copy(
            src_ref=feat_out.at[t],
            dst_ref=feat_in.at[side],
            send_sem=feat_send.at[t],
            recv_sem=feat_recv.at[side],
            device_id={"tensor": t},
            device_id_type=MESH,
        )

    rows = feat_out.shape[1]
    for side in range(2):
        @pl.when(me == last[side])
        def _():
            count = len_ref[side].astype(jnp.float32)
            even = acc[pl.ds(0, PROJ, stride=2), :]
            odd = acc[pl.ds(1, PROJ, stride=2), :]
            low = lax.broadcasted_iota(jnp.int32, (PROJ // 2, 128), 1) < PROJ
            up = jnp.where(low, even[: PROJ // 2], pltpu.roll(odd, PROJ, 1)[: PROJ // 2])
            down = jnp.where(low, pltpu.roll(even, PROJ, 1)[PROJ // 2 :], odd[PROJ // 2 :])
            features = jnp.concatenate([up, down], axis=0) / count
            for t in range(n):
                feat_out[t] = features[t * rows : (t + 1) * rows]
            for t in range(n):
                if t != last[side]:
                    feat_copy(side, t).start()
            feat_in[side] = feat_out[last[side]]

        @pl.when(me != last[side])
        def _():
            feat_copy(side, me).wait_recv()

    for side in range(2):
        for r in range(rows):
            flat[side : side + 1, r * 128 : (r + 1) * 128] = feat_in[side, r : r + 1, :]
    features = flat[...].astype(jnp.bfloat16)
    bank_copy.wait()

    def part_copy(j):
        t = lax.rem(me + j, n)
        return pltpu.make_async_remote_copy(
            src_ref=part.at[t],
            dst_ref=part_in.at[me],
            send_sem=part_send.at[j],
            recv_sem=part_recv.at[me],
            device_id={"tensor": t},
            device_id_type=MESH,
        )

    for j in [*range(1, n), 0]:
        t = lax.rem(me + j, n)
        scores = lax.dot_general(
            bank[pl.ds(pl.multiple_of(t * queries, queries), queries), :], features,
            (((1,), (1,)), ((), ())), preferred_element_type=jnp.float32,
        )
        part[t] = scores.T
        if j:
            part_copy(j).start()
    total = part[me]
    for j in range(1, n):
        source = lax.rem(me + j, n)
        pltpu.make_async_remote_copy(
            src_ref=part.at[source],
            dst_ref=part_in.at[source],
            send_sem=part_send.at[j],
            recv_sem=part_recv.at[source],
            device_id={"tensor": source},
            device_id_type=MESH,
        ).wait_recv()
        total = total + part_in[source]
    out_ref[...] = total[: out_ref.shape[0]]

    for side in range(2):
        @pl.when(me != last[side])
        def _():
            def sent(k, carry):
                chain_copy(side, k).wait_send()
                return carry

            lax.fori_loop(0, chunks, sent, 0)

        @pl.when(me == last[side])
        def _():
            for t in range(n):
                if t != last[side]:
                    feat_copy(side, t).wait_send()
    for j in range(1, n):
        part_copy(j).wait_send()


def per_device(n, x_up, g_up, h_down, g_down, proj_model, proj_hidden, lengths, bank):
    chunks = x_up.shape[0] // (2 * CHUNK)
    nq, feat_dev = bank.shape
    bf16, f32 = jnp.bfloat16, jnp.float32
    dma = pltpu.SemaphoreType.DMA
    hbm = pl.BlockSpec(memory_space=pl.ANY)
    tall = 2 * CHUNK
    return pl.pallas_call(
        functools.partial(kernel, n),
        out_shape=jax.ShapeDtypeStruct((lengths.shape[0], nq // n), f32),
        in_specs=[hbm] * 6 + [pl.BlockSpec(memory_space=pltpu.SMEM), hbm],
        out_specs=pl.BlockSpec(memory_space=pltpu.VMEM),
        scratch_shapes=[
            pltpu.VMEM((chunks, tall, x_up.shape[1]), bf16),
            pltpu.VMEM((chunks, tall, g_up.shape[1]), bf16),
            pltpu.VMEM((chunks, tall, h_down.shape[1]), bf16),
            pltpu.VMEM((chunks, tall, g_down.shape[1]), bf16),
            pltpu.VMEM(proj_model.shape, bf16),
            pltpu.VMEM(proj_hidden.shape, bf16),
            pltpu.VMEM(bank.shape, bf16),
            pltpu.VMEM((2, chunks, CHUNK, 256), f32),
            pltpu.VMEM((2, chunks, CHUNK, 256), f32),
            pltpu.VMEM((128, 128), f32),
            pltpu.VMEM((n, feat_dev // 128, 128), f32),
            pltpu.VMEM((2, feat_dev // 128, 128), f32),
            pltpu.VMEM((8, feat_dev), f32),
            pltpu.VMEM((n, 8, nq // n), f32),
            pltpu.VMEM((n, 8, nq // n), f32),
            dma((8, chunks)),
            dma((3,)),
            dma((2, chunks)),
            dma((2, chunks)),
            dma((n,)),
            dma((2,)),
            dma((n,)),
            dma((n,)),
        ],
        compiler_params=pltpu.CompilerParams(
            collective_id=0, has_side_effects=True, vmem_limit_bytes=58 * 1024 * 1024
        ),
        name="grad_scores",
    )(x_up, g_up, h_down, g_down, proj_model, proj_hidden, lengths, bank)


def solution(mesh):
    in_specs = (
        P(("parts", "dp"), "tensor"),
        P(("parts", "dp"), "tensor"),
        P(("parts", "dp"), "tensor"),
        P(("parts", "dp"), "tensor"),
        P("tensor", None),
        P("tensor", None),
        P(("parts", "dp")),
        P(None, "tensor"),
    )
    return jax.shard_map(
        functools.partial(per_device, mesh.shape["tensor"]),
        mesh=mesh,
        in_specs=in_specs,
        out_specs=P(("parts", "dp"), "tensor"),
        check_vma=False,
    )
```
